32 devices in a mesh: groups: 2 (over x), img: 16 (over z, y, core).
Axes of the slice: x: 2, y: 2, z: 4, core: 2. Of those that a mesh axis runs over, the one named last changes fastest.
Arguments:
- descriptors: bfloat16 [32, 256, 1024], P(('groups', 'img')), parts along dimension 0, may hold values from -6 to 6
- attributes: bfloat16 [32, 3, 1024], P(('groups', 'img')), parts along dimension 0, may hold values from -1 to 4, as said below
- counts: int32 [32], P('groups'), parts along dimension 0, may hold values from 256 to 1024
- owner_slot: int32 [32], P('groups'), parts along dimension 0, may hold values from 0 to 15, as said below
- pair_list: int32 [32, 2], P(('groups', 'img')), parts along dimension 0, may hold values from 0 to 15, as said below
Outputs:
- match_xy: float32 [32, 2, 1024], P(('groups', 'img')), parts along dimension 0
- col_lse: float32 [32, 1024], P(('groups', 'img')), parts along dimension 0
- col_xy: float32 [32, 2, 1024], P(('groups', 'img')), parts along dimension 0
The draws below stay inside these ranges and needn't reach their ends.
There are 2 independent parts, one for each index of `groups`. The reference program is written for one: setup_inputs(seed, part) draws one part's arguments, and reference() takes and returns one part's arrays. A program takes and returns all parts, laid end to end along the dimension named above; each array names one. Nothing has to cross between parts.
Inputs may be any that keep to these rules, and one draw needn't show every extreme that they name: owner_slot is a permutation: every slot holds exactly one image id; slot s lies on the device of index s. The query image of row p is stored on the device that holds row p: owner_slot[pair_list[p,0]] == p; the partner differs from the query. `attributes`: scales lie in 0.5 to 4, coordinates in -1 to 1.
All inputs are finite; a program needn't handle non-finite values.
Results may differ from the reference program's by a relative error of at most 0.0003.
Values may be sent and summed in bfloat16 or wider, within the bound.
No kernel may reach another device: no remote copies, remote signals or barrier semaphores. Data moves between devices by JAX's collectives and lax.ppermute only.
A program may use at most 64 MiB of HBM per device.

```python
import math
import jax
import jax.numpy as jnp
from jax import lax

D = 256
KP = 1024
IMG_DEV = 1
PAIR_DEV = 1
IMAGES = 16
PAIRS = 16


def slot_table(key):
    return jax.random.permutation(jax.random.fold_in(key, 11), IMAGES).astype(jnp.int32)


def draw_owner_slot(key, part):
    return slot_table(key)


def draw_pair_list(key, part):
    slot_of = slot_table(key)
    stored = jnp.argsort(slot_of).astype(jnp.int32)
    row_ids = jnp.arange(PAIRS, dtype=jnp.int32)
    slot_ids = row_ids // PAIR_DEV * IMG_DEV + row_ids % IMG_DEV
    first_ids = stored[slot_ids]
    hot_ids = jax.random.randint(jax.random.fold_in(key, 12), (4,), 0, IMAGES)
    hot_pick = jax.random.randint(jax.random.fold_in(key, 13), (PAIRS,), 0, 4)
    spread_ids = jax.random.randint(jax.random.fold_in(key, 14), (PAIRS,), 0, IMAGES)
    coin_flip = jax.random.randint(jax.random.fold_in(key, 15), (PAIRS,), 0, 2)
    second_ids = jnp.where(coin_flip == 1, hot_ids[hot_pick], spread_ids)
    second_ids = jnp.where(second_ids == first_ids, (first_ids + 1) % IMAGES, second_ids)
    return jnp.stack([first_ids, second_ids], axis=1).astype(jnp.int32)


def draw_descriptors(key, part):
    normal_part = jax.random.normal(jax.random.fold_in(key, 21), (IMAGES, D, KP), jnp.float32)
    shared = jax.random.normal(jax.random.fold_in(key, 22), (1, D, 1), jnp.float32)
    strength = jax.random.uniform(jax.random.fold_in(key, 23), (IMAGES, 1, 4), jnp.float32, 1.5, 2.2)
    aligned = strength * shared + 0.1 * normal_part[:, :, :4]
    normal_part = jnp.concatenate([aligned, normal_part[:, :, 4:]], axis=2)
    return jnp.clip(normal_part, -6.0, 6.0).astype(jnp.bfloat16)


def draw_attributes(key, part):
    kp_scale = jnp.exp(jax.random.uniform(jax.random.fold_in(key, 31), (IMAGES, 1, KP), jnp.float32, math.log(0.5), math.log(2.0)))
    lifted = jax.random.uniform(jax.random.fold_in(key, 32), (IMAGES, 1, 4), jnp.float32, 3.5, 4.0)
    kp_scale = jnp.concatenate([lifted, kp_scale[:, :, 4:]], axis=2)
    placed = jax.random.uniform(jax.random.fold_in(key, 33), (IMAGES, 2, KP), jnp.float32, -1.0, 1.0)
    return jnp.concatenate([kp_scale, placed], axis=1).astype(jnp.bfloat16)


def place_ends(drawn, rng, smallest, largest):
    longest = drawn.shape.index(max(drawn.shape))
    spots = []
    for shift in (0, 1):
        where = [jax.random.randint(jax.random.fold_in(rng, axis), (), 0, length) for axis, length in enumerate(drawn.shape)]
        where[longest] = (where[longest] + shift) % drawn.shape[longest]
        spots.append(tuple(where))
    return drawn.at[spots[0]].set(smallest).at[spots[1]].set(largest)


def setup_inputs(seed: int = 0, part: int = 0) -> dict:
    key_list = jax.random.split(jax.random.key(seed), 6)
    part_keys = jax.random.split(jax.random.fold_in(key_list[5], part), 6)
    return {
        "descriptors": draw_descriptors(jax.random.fold_in(jax.random.fold_in(key_list[5], part), 71), part),
        "attributes": draw_attributes(jax.random.fold_in(jax.random.fold_in(key_list[5], part), 71), part),
        "counts": place_ends(jax.random.randint(part_keys[2], (IMAGES,), KP // 4, KP + 1), jax.random.fold_in(part_keys[2], 1), KP // 4, KP).astype(jnp.int32),
        "owner_slot": draw_owner_slot(jax.random.fold_in(jax.random.fold_in(key_list[5], part), 71), part),
        "pair_list": draw_pair_list(jax.random.fold_in(jax.random.fold_in(key_list[5], part), 71), part),
    }


far_low = -1e+30

def pair_terms(own_desc, own_attr, own_count, other_desc, other_attr, other_count):
    inv_root = 1.0 / math.sqrt(D)
    raw_scores = lax.dot_general(own_desc, other_desc, (((0,), (0,)), ((), ())), preferred_element_type=jnp.float32)
    own_scale = own_attr[0].astype(jnp.float32) * inv_root
    other_scale = other_attr[0].astype(jnp.float32)
    scores = raw_scores * own_scale[:, None] * other_scale[None, :]
    column_ix = jnp.arange(KP, dtype=jnp.int32)
    row_valid = column_ix < own_count
    col_valid = column_ix < other_count
    row_max = lax.optimization_barrier(jnp.max(jnp.where(col_valid[None, :], scores, far_low), axis=1))
    row_weights = jnp.where(col_valid[None, :], jnp.exp(scores - row_max[:, None]), 0.0)
    row_probs = row_weights / lax.optimization_barrier(jnp.sum(row_weights, axis=1))[:, None]
    matched = jnp.dot(other_attr[1:].astype(jnp.float32), row_probs.T, precision=lax.Precision.HIGHEST)
    matched = jnp.where(row_valid[None, :], matched, 0.0)
    col_top = lax.optimization_barrier(jnp.max(jnp.where(row_valid[:, None], scores, far_low), axis=0))
    col_weights = jnp.where(row_valid[:, None], jnp.exp(scores - col_top[None, :]), 0.0)
    col_total = lax.optimization_barrier(jnp.sum(col_weights, axis=0))
    col_spot = jnp.dot(own_attr[1:].astype(jnp.float32), col_weights, precision=lax.Precision.HIGHEST)
    return (matched, col_top, col_total, col_spot)

def reference(descriptors, attributes, counts, owner_slot, pair_list):
    first_slot = owner_slot[pair_list[:, 0]].astype(jnp.int32)
    second_slot = owner_slot[pair_list[:, 1]].astype(jnp.int32)

    def one_pair(which):
        qa = first_slot[which]
        qb = second_slot[which]
        return pair_terms(descriptors[qa], attributes[qa], counts[pair_list[which, 0]], descriptors[qb], attributes[qb], counts[pair_list[which, 1]])
    matched, col_top, col_total, col_spot = lax.map(one_pair, jnp.arange(PAIRS, dtype=jnp.int32))

    def merge_slot(slot_id):
        hit_mask = second_slot == slot_id
        col_peak = lax.optimization_barrier(jnp.max(jnp.where(hit_mask[:, None], col_top, far_low), axis=0))
        col_peak = jnp.maximum(col_peak, 0.0)
        fade_factor = jnp.where(hit_mask[:, None], jnp.exp(col_top - col_peak[None, :]), 0.0)
        partition = jnp.exp(-col_peak) + lax.optimization_barrier(jnp.sum(fade_factor * col_total, axis=0))
        soft_xy = lax.optimization_barrier(jnp.sum(fade_factor[:, None, :] * col_spot, axis=0)) / partition[None, :]
        return (col_peak + jnp.log(partition), soft_xy)
    log_total, soft_xy = lax.map(merge_slot, jnp.arange(IMAGES, dtype=jnp.int32))
    return (matched, log_total, soft_xy)
```

```python
import functools
import math

import jax
import jax.numpy as jnp
from jax import lax
from jax.experimental import pallas as pl
from jax.experimental.pallas import tpu as pltpu
from jax.sharding import PartitionSpec as P

LOW = -1e30
LANES = 128
ROWS = 16
VMEM = pl.BlockSpec(memory_space=pltpu.VMEM)
SMEM = pl.BlockSpec(memory_space=pltpu.SMEM)
ANY = pl.BlockSpec(memory_space=pl.ANY)
PARAMS = pltpu.CompilerParams(vmem_limit_bytes=32 * 1024 * 1024)


def pack(pairs, owners, desc, attr, out):
    row_tiles, per, rows, _ = out.shape
    col_tiles = desc.shape[2] // LANES
    each = rows // ROWS - 1
    for c in range(col_tiles):
        at = c % each * ROWS
        out[:, c // each, at : at + ROWS, :] = desc[:, :, c * LANES : (c + 1) * LANES]
    slot = owners[pairs[0, 1]].astype(jnp.float32)
    pad = jnp.full((ROWS - 3, LANES), slot, jnp.float32).astype(out.dtype)
    tails = [
        jnp.concatenate([attr[:, c * LANES : (c + 1) * LANES], pad], axis=0)
        for c in range(col_tiles)
    ]
    for r in range(row_tiles):
        for q in range(per):
            out[r, q, rows - ROWS :, :] = tails[(r * per + q) % col_tiles]


def pick(got, out):
    n, rows, _ = got.shape
    slots = [
        jnp.max(got[p, rows - ROWS :, :].astype(jnp.float32)[3:4, :]).astype(jnp.int32)
        for p in range(n)
    ]
    for p in range(n):
        out[p] = got[slots[p]]


def column_block(got, b):
    row_tiles, per, rows, _ = got.shape
    each = rows // ROWS - 1
    tiles, rest = [], []
    for c in (2 * b, 2 * b + 1):
        at = c % each * ROWS
        tile = got[:, c // each, at : at + ROWS, :]
        tiles.append(tile.reshape(row_tiles * ROWS, LANES))
        rest.append(got[c // per, c % per, rows - ROWS :, :].astype(jnp.float32)[:3, :])
    return jnp.concatenate(tiles, axis=1), jnp.concatenate(rest, axis=1)


def softmax_sums(left, left_cols, left_count, right, right_scale, scores):
    height = left.shape[0]
    step = 256
    top = None
    for r in range(0, height, step):
        raw = jnp.dot(left[r : r + step, :], right, preferred_element_type=jnp.float32)
        row = r + lax.broadcasted_iota(jnp.int32, (step, 1), 0)
        part = raw * left_cols[r : r + step, 0:1] * right_scale
        part = jnp.where(row < left_count, part, LOW)
        scores[r : r + step, :] = part
        best = jnp.max(part, axis=0, keepdims=True)
        top = best if top is None else jnp.maximum(top, best)
    total = spot_x = spot_y = 0.0
    for r in range(0, height, step):
        weight = jnp.exp2(scores[r : r + step, :] - top)
        total += jnp.sum(weight, axis=0, keepdims=True)
        spot_x += jnp.sum(weight * left_cols[r : r + step, 1:2], axis=0, keepdims=True)
        spot_y += jnp.sum(weight * left_cols[r : r + step, 2:3], axis=0, keepdims=True)
    return top, total, spot_x, spot_y


def column_kernel(factor, pairs, owners, counts, left, left_cols, got, out, scores, packed):
    keypoints = left.shape[0]
    count = counts[pairs[0, 0]]
    blocks = keypoints // LANES
    for b in range(keypoints // 256):
        right, rest = column_block(got, b)
        top, total, spot_x, spot_y = softmax_sums(
            left, left_cols, count, right, rest[0:1] * factor, scores
        )
        lse = top + jnp.log2(total)
        for h in range(2):
            c = 2 * b + h
            cut = slice(h * LANES, (h + 1) * LANES)
            packed[c : c + 1, :] = lse[:, cut]
            packed[blocks + c : blocks + c + 1, :] = (spot_x / total)[:, cut]
            packed[2 * blocks + c : 2 * blocks + c + 1, :] = (spot_y / total)[:, cut]
    row = lax.broadcasted_iota(jnp.int32, packed.shape, 0)
    out[...] = jnp.broadcast_to(jnp.where(row < blocks, LOW, 0.0), out.shape)
    out[owners[pairs[0, 1]]] = packed[...]


def row_kernel(factor, pairs, counts, desc, attr, got, out, scores, left, left_cols):
    keypoints = desc.shape[1]
    for b in range(keypoints // 256):
        block, rest = column_block(got, b)
        left[b * 256 : (b + 1) * 256, :] = block.astype(jnp.float32).T.astype(left.dtype)
        fill = jnp.zeros((5, 256), jnp.float32)
        left_cols[b * 256 : (b + 1) * 256, :] = jnp.concatenate([rest, fill], axis=0).T
    for b in range(keypoints // 256):
        cut = slice(b * 256, (b + 1) * 256)
        scale = attr[0:1, cut].astype(jnp.float32) * factor
        _, total, spot_x, spot_y = softmax_sums(
            left, left_cols, counts[pairs[0, 1]], desc[:, cut], scale, scores
        )
        col = b * 256 + lax.broadcasted_iota(jnp.int32, (1, 256), 1)
        valid = col < counts[pairs[0, 0]]
        out[0, 0:1, cut] = jnp.where(valid, spot_x / total, 0.0)
        out[0, 1:2, cut] = jnp.where(valid, spot_y / total, 0.0)


def merge_kernel(got, lse_out, xy_out):
    n, rows, _ = got.shape
    blocks = rows // 3
    lse = got[:, :blocks, :]
    peak = jnp.maximum(jnp.max(lse, axis=0), 0.0)
    share = jnp.exp2(lse - peak[None])
    partition = jnp.exp2(-peak) + jnp.sum(share, axis=0)
    log_total = (peak + jnp.log2(partition)) * math.log(2.0)
    x = jnp.sum(share * got[:, blocks : 2 * blocks, :], axis=0) / partition
    y = jnp.sum(share * got[:, 2 * blocks :, :], axis=0) / partition
    for c in range(blocks):
        cut = slice(c * LANES, (c + 1) * LANES)
        lse_out[0:1, cut] = log_total[c : c + 1]
        xy_out[0, 0:1, cut] = x[c : c + 1]
        xy_out[0, 1:2, cut] = y[c : c + 1]


def shards(descriptors, attributes, counts, owner_slot, pair_list):
    n = lax.axis_size("img")
    _, width, keypoints = descriptors.shape
    row_tiles, col_tiles = width // ROWS, keypoints // LANES
    each = row_tiles * col_tiles // n
    per = n // row_tiles
    rows = (each + 1) * ROWS
    factor = math.log2(math.e) / math.sqrt(width)
    bf16, f32 = jnp.bfloat16, jnp.float32
    desc, attr = descriptors[0], attributes[0]
    share = functools.partial(
        lax.all_to_all, axis_name="img", split_axis=0, concat_axis=0, tiled=True
    )
    call = functools.partial(pl.pallas_call, compiler_params=PARAMS)
    shape = jax.ShapeDtypeStruct
    sent = call(
        pack,
        out_shape=shape((row_tiles, per, rows, LANES), bf16),
        in_specs=[SMEM, SMEM, VMEM, VMEM],
        out_specs=VMEM,
        name="pack",
    )(pair_list, owner_slot, desc.reshape(row_tiles, ROWS, keypoints), attr)
    spread = share(sent.reshape(n, rows, LANES))
    chosen = call(
        pick, out_shape=shape((n, rows, LANES), bf16), in_specs=[VMEM], out_specs=VMEM, name="pick"
    )(spread)
    partner = share(chosen).reshape(row_tiles, per, rows, LANES)
    left = desc.T
    left_cols = attr.T.astype(f32)
    scores = pltpu.VMEM((keypoints, 256), f32)
    partials = call(
        functools.partial(column_kernel, factor),
        out_shape=shape((n, 3 * col_tiles, LANES), f32),
        in_specs=[SMEM, SMEM, SMEM, VMEM, VMEM, VMEM],
        out_specs=VMEM,
        scratch_shapes=[scores, pltpu.VMEM((3 * col_tiles, LANES), f32)],
        name="columns",
    )(pair_list, owner_slot, counts, left, left_cols, partner)
    arrived = share(partials)
    matched = call(
        functools.partial(row_kernel, factor),
        out_shape=shape((1, 2, keypoints), f32),
        in_specs=[SMEM, SMEM, VMEM, VMEM, VMEM],
        out_specs=VMEM,
        scratch_shapes=[
            scores,
            pltpu.VMEM((keypoints, width), bf16),
            pltpu.VMEM((keypoints, 8), f32),
        ],
        cost_estimate=pl.CostEstimate(
            flops=2 * keypoints * keypoints * width,
            bytes_accessed=4 * keypoints * width,
            transcendentals=keypoints * keypoints,
        ),
        name="rows",
    )(pair_list, counts, desc, attr, partner)
    log_total, soft_xy = call(
        merge_kernel,
        out_shape=(shape((1, keypoints), f32), shape((1, 2, keypoints), f32)),
        in_specs=[VMEM],
        out_specs=(VMEM, VMEM),
        name="merge",
    )(arrived)
    return matched, log_total, soft_xy


def solution(mesh):
    both = ("groups", "img")
    return jax.shard_map(
        shards,
        mesh=mesh,
        in_specs=(P(both, None, None), P(both, None, None), P("groups"), P("groups"), P(both, None)),
        out_specs=(P(both, None, None), P(both, None), P(both, None, None)),
        check_vma=False,
    )
```

```python
import functools
import math

import jax
import jax.numpy as jnp
from jax import lax
from jax.experimental import pallas as pl
from jax.experimental.pallas import tpu as pltpu
from jax.sharding import PartitionSpec as P

LOW = -1e30
LANES = 128
ROWS = 16
TAIL = 8
VMEM = pl.BlockSpec(memory_space=pltpu.VMEM)
SMEM = pl.BlockSpec(memory_space=pltpu.SMEM)
ANY = pl.BlockSpec(memory_space=pl.ANY)
MIB = 1024 * 1024
PARAMS = pltpu.CompilerParams(vmem_limit_bytes=32 * MIB)
WIDE = pltpu.CompilerParams(vmem_limit_bytes=58 * MIB)


def pack(pairs, owners, counts, desc, attr, out, meta, pair_s, owner_s, count_s, attr_s, done):
    row_tiles, per, rows, _ = out.shape
    col_tiles = desc.shape[2] // LANES
    each = rows // ROWS
    small = [
        pltpu.make_async_copy(a, b, done.at[i])
        for i, (a, b) in enumerate(
            ((pairs, pair_s), (owners, owner_s), (counts, count_s), (attr, attr_s))
        )
    ]
    for copy in small:
        copy.start()
    large = [
        pltpu.make_async_copy(
            desc.at[:, :, pl.ds(c * LANES, LANES)],
            out.at[:, c // each, pl.ds(c % each * ROWS, ROWS), :],
            done.at[4 + c],
        )
        for c in range(col_tiles)
    ]
    for copy in large:
        copy.start()
    for copy in small:
        copy.wait()
    slot = owner_s[pair_s[0, 1]]
    row = lax.broadcasted_iota(jnp.int32, meta.shape, 0)
    theirs = jnp.where(row == 1, count_s[pair_s[0, 0]], count_s[pair_s[0, 1]])
    meta[...] = jnp.where(row == 0, slot, theirs)
    pad = jnp.full((TAIL - 3, LANES), slot.astype(jnp.float32), jnp.float32).astype(out.dtype)
    tails = [
        jnp.concatenate([attr_s[0, :, c * LANES : (c + 1) * LANES], pad], axis=0)
        for c in range(col_tiles)
    ]
    for r in range(row_tiles):
        for q in range(per):
            out[r, q, rows - TAIL :, :] = tails[(r * per + q) % col_tiles]
    for copy in large:
        copy.wait()


def pick(got, out):
    n, rows, _ = got.shape
    slots = [got[p, rows - TAIL :, :].astype(jnp.float32)[3, 0].astype(jnp.int32) for p in range(n)]
    for p in range(n):
        out[p] = got[slots[p]]


def column_block(got, b):
    row_tiles, per, rows, _ = got.shape
    each = rows // ROWS
    tiles, rest = [], []
    for c in (2 * b, 2 * b + 1):
        at = c % each * ROWS
        tile = got[:, c // each, at : at + ROWS, :]
        tiles.append(tile.reshape(row_tiles * ROWS, LANES))
        rest.append(got[c // per, c % per, rows - TAIL :, :].astype(jnp.float32)[:3, :])
    return jnp.concatenate(tiles, axis=1), jnp.concatenate(rest, axis=1)


def softmax_sums(left, left_cols, left_count, right, right_scale, scores):
    height = left.shape[0]
    step = 256
    top = None
    for r in range(0, height, step):
        raw = jnp.dot(left[r : r + step, :], right, preferred_element_type=jnp.float32)
        row = r + lax.broadcasted_iota(jnp.int32, (step, 1), 0)
        part = raw * left_cols[r : r + step, 0:1] * right_scale
        part = jnp.where(row < left_count, part, LOW)
        scores[r : r + step, :] = part
        best = jnp.max(part, axis=0, keepdims=True)
        top = best if top is None else jnp.maximum(top, best)
    total = spot_x = spot_y = 0.0
    for r in range(0, height, step):
        weight = jnp.exp2(scores[r : r + step, :] - top)
        total += jnp.sum(weight, axis=0, keepdims=True)
        spot_x += jnp.sum(weight * left_cols[r : r + step, 1:2], axis=0, keepdims=True)
        spot_y += jnp.sum(weight * left_cols[r : r + step, 2:3], axis=0, keepdims=True)
    return top, total, spot_x, spot_y


def column_kernel(factor, meta, left, left_cols, got, out, scores, packed):
    keypoints = left.shape[0]
    count = meta[1:2, 0:1]
    blocks = keypoints // LANES
    for b in range(keypoints // 256):
        right, rest = column_block(got, b)
        top, total, spot_x, spot_y = softmax_sums(
            left, left_cols, count, right, rest[0:1] * factor, scores
        )
        lse = top + jnp.log2(total)
        for h in range(2):
            c = 2 * b + h
            cut = slice(h * LANES, (h + 1) * LANES)
            packed[c : c + 1, :] = lse[:, cut]
            packed[blocks + c : blocks + c + 1, :] = (spot_x / total)[:, cut]
            packed[2 * blocks + c : 2 * blocks + c + 1, :] = (spot_y / total)[:, cut]
    row = lax.broadcasted_iota(jnp.int32, packed.shape, 0)
    none = jnp.where(row < blocks, LOW, 0.0)
    for s in range(out.shape[0]):
        out[s] = jnp.where(meta[0:1, :] == s, packed[...], none)


def row_kernel(factor, meta, desc, attr, got, out, scores, left, left_cols):
    keypoints = desc.shape[1]
    for b in range(keypoints // 256):
        block, rest = column_block(got, b)
        left[b * 256 : (b + 1) * 256, :] = block.astype(jnp.float32).T.astype(left.dtype)
        fill = jnp.zeros((5, 256), jnp.float32)
        left_cols[b * 256 : (b + 1) * 256, :] = jnp.concatenate([rest, fill], axis=0).T
    for b in range(keypoints // 256):
        cut = slice(b * 256, (b + 1) * 256)
        scale = attr[0, 0:1, cut].astype(jnp.float32) * factor
        _, total, spot_x, spot_y = softmax_sums(
            left, left_cols, meta[2:3, 0:1], desc[:, cut], scale, scores
        )
        col = b * 256 + lax.broadcasted_iota(jnp.int32, (1, 256), 1)
        valid = col < meta[1:2, 0:1]
        out[0, 0:1, cut] = jnp.where(valid, spot_x / total, 0.0)
        out[0, 1:2, cut] = jnp.where(valid, spot_y / total, 0.0)


def merge_kernel(got, lse_out, xy_out):
    n, rows, _ = got.shape
    blocks = rows // 3
    lse = got[:, :blocks, :]
    peak = jnp.maximum(jnp.max(lse, axis=0), 0.0)
    share = jnp.exp2(lse - peak[None])
    partition = jnp.exp2(-peak) + jnp.sum(share, axis=0)
    log_total = (peak + jnp.log2(partition)) * math.log(2.0)
    x = jnp.sum(share * got[:, blocks : 2 * blocks, :], axis=0) / partition
    y = jnp.sum(share * got[:, 2 * blocks :, :], axis=0) / partition
    for c in range(blocks):
        cut = slice(c * LANES, (c + 1) * LANES)
        lse_out[0:1, cut] = log_total[c : c + 1]
        xy_out[0, 0:1, cut] = x[c : c + 1]
        xy_out[0, 1:2, cut] = y[c : c + 1]


def shards(descriptors, attributes, counts, owner_slot, pair_list):
    n = lax.axis_size("img")
    _, width, keypoints = descriptors.shape
    row_tiles, col_tiles = width // ROWS, keypoints // LANES
    each = row_tiles * col_tiles // n
    per = n // row_tiles
    rows = each * ROWS + TAIL
    factor = math.log2(math.e) / math.sqrt(width)
    bf16, f32 = jnp.bfloat16, jnp.float32
    desc, attr = descriptors[0], attributes[0]
    share = functools.partial(
        lax.all_to_all, axis_name="img", split_axis=0, concat_axis=0, tiled=True
    )

    def call(*args, compiler_params=PARAMS, **kwargs):
        return pl.pallas_call(*args, compiler_params=compiler_params, **kwargs)

    shape = jax.ShapeDtypeStruct
    sent, meta = call(
        pack,
        out_shape=(pltpu.VMEM((row_tiles, per, rows, LANES), bf16), pltpu.VMEM((8, LANES), jnp.int32)),
        in_specs=[ANY] * 5,
        out_specs=(VMEM, VMEM),
        scratch_shapes=[
            pltpu.SMEM(pair_list.shape, jnp.int32),
            pltpu.SMEM(owner_slot.shape, jnp.int32),
            pltpu.SMEM(counts.shape, jnp.int32),
            pltpu.VMEM(attributes.shape, bf16),
            pltpu.SemaphoreType.DMA((4 + col_tiles,)),
        ],
        compiler_params=WIDE,
        name="pack",
    )(pair_list, owner_slot, counts, desc.reshape(row_tiles, ROWS, keypoints), attributes)
    spread = share(sent.reshape(n, rows, LANES))
    chosen = call(
        pick, out_shape=pltpu.VMEM((n, rows, LANES), bf16), in_specs=[VMEM], out_specs=VMEM, name="pick"
    )(spread)
    partner = share(chosen).reshape(row_tiles, per, rows, LANES)
    left = desc.T
    left_cols = attr.T.astype(f32)
    scores = pltpu.VMEM((keypoints, 256), f32)
    partials = call(
        functools.partial(column_kernel, factor),
        out_shape=pltpu.VMEM((n, 3 * col_tiles, LANES), f32),
        in_specs=[VMEM] * 4,
        out_specs=VMEM,
        scratch_shapes=[scores, pltpu.VMEM((3 * col_tiles, LANES), f32)],
        name="columns",
    )(meta, left, left_cols, partner)
    arrived = share(partials)
    matched = call(
        functools.partial(row_kernel, factor),
        out_shape=shape((1, 2, keypoints), f32),
        in_specs=[VMEM] * 4,
        out_specs=VMEM,
        scratch_shapes=[
            scores,
            pltpu.VMEM((keypoints, width), bf16),
            pltpu.VMEM((keypoints, 8), f32),
        ],
        cost_estimate=pl.CostEstimate(
            flops=2 * keypoints * keypoints * width,
            bytes_accessed=4 * keypoints * width,
            transcendentals=keypoints * keypoints,
        ),
        name="rows",
    )(meta, desc, attributes, partner)
    log_total, soft_xy = call(
        merge_kernel,
        out_shape=(shape((1, keypoints), f32), shape((1, 2, keypoints), f32)),
        in_specs=[VMEM],
        out_specs=(VMEM, VMEM),
        name="merge",
    )(arrived)
    return matched, log_total, soft_xy


def solution(mesh):
    both = ("groups", "img")
    return jax.shard_map(
        shards,
        mesh=mesh,
        in_specs=(P(both, None, None), P(both, None, None), P("groups"), P("groups"), P(both, None)),
        out_specs=(P(both, None, None), P(both, None), P(both, None, None)),
        check_vma=False,
    )
```

```python
import functools
import math

import jax
import jax.numpy as jnp
from jax import lax
from jax.experimental import pallas as pl
from jax.experimental.pallas import tpu as pltpu
from jax.sharding import PartitionSpec as P

LOW = -1e30
LANES = 128
ROWS = 16
TAIL = 8
VMEM = pl.BlockSpec(memory_space=pltpu.VMEM)
SMEM = pl.BlockSpec(memory_space=pltpu.SMEM)
ANY = pl.BlockSpec(memory_space=pl.ANY)
MIB = 1024 * 1024
PARAMS = pltpu.CompilerParams(vmem_limit_bytes=32 * MIB)
WIDE = pltpu.CompilerParams(vmem_limit_bytes=58 * MIB)


def pack(pairs, owners, counts, desc, attr, out, meta, pair_s, owner_s, count_s, attr_s, done):
    row_tiles, per, rows, _ = out.shape
    col_tiles = desc.shape[2] // LANES
    each = rows // ROWS
    small = [
        pltpu.make_async_copy(a, b, done.at[i])
        for i, (a, b) in enumerate(
            ((pairs, pair_s), (owners, owner_s), (counts, count_s), (attr, attr_s))
        )
    ]
    for copy in small:
        copy.start()
    large = [
        pltpu.make_async_copy(
            desc.at[:, :, pl.ds(c * LANES, LANES)],
            out.at[:, c // each, pl.ds(c % each * ROWS, ROWS), :],
            done.at[4 + c],
        )
        for c in range(col_tiles)
    ]
    for copy in large:
        copy.start()
    for copy in small:
        copy.wait()
    slot = owner_s[pair_s[0, 1]]
    row = lax.broadcasted_iota(jnp.int32, meta.shape, 0)
    theirs = jnp.where(row == 1, count_s[pair_s[0, 0]], count_s[pair_s[0, 1]])
    meta[...] = jnp.where(row == 0, slot, theirs)
    pad = jnp.full((TAIL - 3, LANES), slot.astype(jnp.float32), jnp.float32).astype(out.dtype)
    tails = [
        jnp.concatenate([attr_s[0, :, c * LANES : (c + 1) * LANES], pad], axis=0)
        for c in range(col_tiles)
    ]
    for r in range(row_tiles):
        for q in range(per):
            out[r, q, rows - TAIL :, :] = tails[(r * per + q) % col_tiles]
    for copy in large:
        copy.wait()


def pick(got, out):
    n, rows, _ = got.shape
    slots = [got[p, rows - TAIL :, :].astype(jnp.float32)[3, 0].astype(jnp.int32) for p in range(n)]
    for p in range(n):
        out[p] = got[slots[p]]


def column_block(got, b):
    row_tiles, per, rows, _ = got.shape
    each = rows // ROWS
    tiles, rest = [], []
    for c in (2 * b, 2 * b + 1):
        at = c % each * ROWS
        tile = got[:, c // each, at : at + ROWS, :]
        tiles.append(tile.reshape(row_tiles * ROWS, LANES))
        rest.append(got[c // per, c % per, rows - TAIL :, :].astype(jnp.float32)[:3, :])
    return jnp.concatenate(tiles, axis=1), jnp.concatenate(rest, axis=1)


def softmax_sums(left, left_cols, right, right_scale, scores):
    height, width = left.shape[0], right.shape[1]
    step = 256

    def rows_of(k, r):
        return jnp.concatenate([left_cols[k, r : r + step, :]] * (width // LANES), axis=1)

    def fold(values, how):
        return how(values.reshape(step // 8, 8, width), axis=0)

    top = None
    for r in range(0, height, step):
        raw = jnp.dot(left[r : r + step, :], right, preferred_element_type=jnp.float32)
        part = raw * rows_of(0, r) * right_scale + rows_of(3, r)
        scores[r : r + step, :] = part
        best = fold(part, jnp.max)
        top = best if top is None else jnp.maximum(top, best)
    top = jnp.max(top, axis=0, keepdims=True)
    sums = [jnp.zeros((8, width), jnp.float32)] * 3
    for r in range(0, height, step):
        weight = jnp.exp2(scores[r : r + step, :] - top)
        parts = (weight, weight * rows_of(1, r), weight * rows_of(2, r))
        sums = [so_far + fold(part, jnp.sum) for so_far, part in zip(sums, parts)]
    return top, *(jnp.sum(part, axis=0, keepdims=True) for part in sums)


def column_kernel(factor, meta, left, left_cols, got, out, scores, packed):
    keypoints = left.shape[0]
    blocks = keypoints // LANES
    for b in range(keypoints // 256):
        right, rest = column_block(got, b)
        top, total, spot_x, spot_y = softmax_sums(left, left_cols, right, rest[0:1] * factor, scores)
        lse = top + jnp.log2(total)
        for h in range(2):
            c = 2 * b + h
            cut = slice(h * LANES, (h + 1) * LANES)
            packed[c : c + 1, :] = lse[:, cut]
            packed[blocks + c : blocks + c + 1, :] = (spot_x / total)[:, cut]
            packed[2 * blocks + c : 2 * blocks + c + 1, :] = (spot_y / total)[:, cut]
    row = lax.broadcasted_iota(jnp.int32, packed.shape, 0)
    none = jnp.where(row < blocks, LOW, 0.0)
    for s in range(out.shape[0]):
        out[s] = jnp.where(meta[0:1, :] == s, packed[...], none)


def row_kernel(factor, meta, desc, attr, got, out, scores, left, left_cols):
    keypoints = desc.shape[1]
    for b in range(keypoints // 256):
        block, rest = column_block(got, b)
        left[b * 256 : (b + 1) * 256, :] = block.astype(jnp.float32).T.astype(left.dtype)
        cols = jnp.concatenate([rest, jnp.zeros((5, 256), jnp.float32)], axis=0).T
        for k in range(3):
            left_cols[k, b * 256 : (b + 1) * 256, :] = jnp.broadcast_to(cols[:, k : k + 1], (256, LANES))
    row = lax.broadcasted_iota(jnp.int32, (keypoints, LANES), 0)
    left_cols[3] = jnp.where(row < meta[2:3, :], 0.0, LOW)
    for b in range(keypoints // 256):
        cut = slice(b * 256, (b + 1) * 256)
        scale = attr[0, 0:1, cut].astype(jnp.float32) * factor
        _, total, spot_x, spot_y = softmax_sums(left, left_cols, desc[:, cut], scale, scores)
        col = b * 256 + lax.broadcasted_iota(jnp.int32, (1, 256), 1)
        valid = col < meta[1:2, 0:1]
        out[0, 0:1, cut] = jnp.where(valid, spot_x / total, 0.0)
        out[0, 1:2, cut] = jnp.where(valid, spot_y / total, 0.0)


def merge_kernel(got, lse_out, xy_out):
    n, rows, _ = got.shape
    blocks = rows // 3
    lse = got[:, :blocks, :]
    peak = jnp.maximum(jnp.max(lse, axis=0), 0.0)
    share = jnp.exp2(lse - peak[None])
    partition = jnp.exp2(-peak) + jnp.sum(share, axis=0)
    log_total = (peak + jnp.log2(partition)) * math.log(2.0)
    x = jnp.sum(share * got[:, blocks : 2 * blocks, :], axis=0) / partition
    y = jnp.sum(share * got[:, 2 * blocks :, :], axis=0) / partition
    for c in range(blocks):
        cut = slice(c * LANES, (c + 1) * LANES)
        lse_out[0:1, cut] = log_total[c : c + 1]
        xy_out[0, 0:1, cut] = x[c : c + 1]
        xy_out[0, 1:2, cut] = y[c : c + 1]


def shards(descriptors, attributes, counts, owner_slot, pair_list):
    n = lax.axis_size("img")
    _, width, keypoints = descriptors.shape
    row_tiles, col_tiles = width // ROWS, keypoints // LANES
    each = row_tiles * col_tiles // n
    per = n // row_tiles
    rows = each * ROWS + TAIL
    factor = math.log2(math.e) / math.sqrt(width)
    bf16, f32 = jnp.bfloat16, jnp.float32
    desc = descriptors[0]
    share = functools.partial(
        lax.all_to_all, axis_name="img", split_axis=0, concat_axis=0, tiled=True
    )

    def call(*args, compiler_params=PARAMS, **kwargs):
        return pl.pallas_call(*args, compiler_params=compiler_params, **kwargs)

    shape = jax.ShapeDtypeStruct
    sent, meta = call(
        pack,
        out_shape=(shape((row_tiles, per, rows, LANES), bf16), shape((8, LANES), jnp.int32)),
        in_specs=[ANY] * 5,
        out_specs=(VMEM, VMEM),
        scratch_shapes=[
            pltpu.SMEM(pair_list.shape, jnp.int32),
            pltpu.SMEM(owner_slot.shape, jnp.int32),
            pltpu.SMEM(counts.shape, jnp.int32),
            pltpu.VMEM(attributes.shape, bf16),
            pltpu.SemaphoreType.DMA((4 + col_tiles,)),
        ],
        compiler_params=WIDE,
        name="pack",
    )(pair_list, owner_slot, counts, desc.reshape(row_tiles, ROWS, keypoints), attributes)
    spread = share(sent.reshape(n, rows, LANES))
    left = desc.T
    spread, left = lax.optimization_barrier((spread, left))
    chosen = call(
        pick, out_shape=shape((n, rows, LANES), bf16), in_specs=[VMEM], out_specs=VMEM, name="pick"
    )(spread)
    chosen, late, meta = lax.optimization_barrier((chosen, attributes, meta))
    here = lax.broadcasted_iota(jnp.int32, (keypoints, LANES), 0) < meta[1:2, :]
    left_cols = jnp.concatenate(
        [
            jnp.broadcast_to(late[0].astype(f32)[:, :, None], (3, keypoints, LANES)),
            jnp.where(here, 0.0, LOW)[None],
        ]
    )
    partner = share(chosen).reshape(row_tiles, per, rows, LANES)
    scores = pltpu.VMEM((keypoints, 256), f32)
    partials = call(
        functools.partial(column_kernel, factor),
        out_shape=pltpu.VMEM((n, 3 * col_tiles, LANES), f32),
        in_specs=[VMEM] * 4,
        out_specs=VMEM,
        scratch_shapes=[scores, pltpu.VMEM((3 * col_tiles, LANES), f32)],
        name="columns",
    )(meta, left, left_cols, partner)
    arrived = share(partials)
    matched = call(
        functools.partial(row_kernel, factor),
        out_shape=shape((1, 2, keypoints), f32),
        in_specs=[VMEM] * 4,
        out_specs=VMEM,
        scratch_shapes=[
            scores,
            pltpu.VMEM((keypoints, width), bf16),
            pltpu.VMEM((4, keypoints, LANES), f32),
        ],
        cost_estimate=pl.CostEstimate(
            flops=2 * keypoints * keypoints * width,
            bytes_accessed=4 * keypoints * width,
            transcendentals=keypoints * keypoints,
        ),
        name="rows",
    )(meta, desc, attributes, partner)
    log_total, soft_xy = call(
        merge_kernel,
        out_shape=(shape((1, keypoints), f32), shape((1, 2, keypoints), f32)),
        in_specs=[VMEM],
        out_specs=(VMEM, VMEM),
        name="merge",
    )(arrived)
    return matched, log_total, soft_xy


def solution(mesh):
    both = ("groups", "img")
    return jax.shard_map(
        shards,
        mesh=mesh,
        in_specs=(P(both, None, None), P(both, None, None), P("groups"), P("groups"), P(both, None)),
        out_specs=(P(both, None, None), P(both, None), P(both, None, None)),
        check_vma=False,
    )
```

```python
import functools
import math

import jax
import jax.numpy as jnp
from jax import lax
from jax.experimental import pallas as pl
from jax.experimental.pallas import tpu as pltpu
from jax.sharding import PartitionSpec as P

LOW = -1e30
LANES = 128
ROWS = 16
TAIL = 8
VMEM = pl.BlockSpec(memory_space=pltpu.VMEM)
SMEM = pl.BlockSpec(memory_space=pltpu.SMEM)
ANY = pl.BlockSpec(memory_space=pl.ANY)
MIB = 1024 * 1024
PARAMS = pltpu.CompilerParams(vmem_limit_bytes=32 * MIB)
WIDE = pltpu.CompilerParams(vmem_limit_bytes=58 * MIB)


def pack(pairs, owners, counts, desc, attr, out, meta, pair_s, owner_s, count_s, attr_s, done):
    row_tiles, per, rows, _ = out.shape
    col_tiles = desc.shape[2] // LANES
    each = rows // ROWS
    small = [
        pltpu.make_async_copy(a, b, done.at[i])
        for i, (a, b) in enumerate(
            ((pairs, pair_s), (owners, owner_s), (counts, count_s), (attr, attr_s))
        )
    ]
    for copy in small:
        copy.start()
    large = [
        pltpu.make_async_copy(
            desc.at[:, :, pl.ds(c * LANES, LANES)],
            out.at[:, c // each, pl.ds(c % each * ROWS, ROWS), :],
            done.at[4 + c],
        )
        for c in range(col_tiles)
    ]
    for copy in large:
        copy.start()
    for copy in small:
        copy.wait()
    slot = owner_s[pair_s[0, 1]]
    row = lax.broadcasted_iota(jnp.int32, meta.shape, 0)
    theirs = jnp.where(row == 1, count_s[pair_s[0, 0]], count_s[pair_s[0, 1]])
    meta[...] = jnp.where(row == 0, slot, theirs)
    pad = jnp.full((TAIL - 3, LANES), slot.astype(jnp.float32), jnp.float32).astype(out.dtype)
    tails = [
        jnp.concatenate([attr_s[0, :, c * LANES : (c + 1) * LANES], pad], axis=0)
        for c in range(col_tiles)
    ]
    for r in range(row_tiles):
        for q in range(per):
            out[r, q, rows - TAIL :, :] = tails[(r * per + q) % col_tiles]
    for copy in large:
        copy.wait()


def pick(got, out):
    n, rows, _ = got.shape
    slots = [got[p, rows - TAIL :, :].astype(jnp.float32)[3, 0].astype(jnp.int32) for p in range(n)]
    for p in range(n):
        out[p] = got[slots[p]]


def column_block(got, b, wide):
    row_tiles, per, rows, _ = got.shape
    each = rows // ROWS
    tiles, rest = [], []
    for c in range(b * wide // LANES, (b + 1) * wide // LANES):
        at = c % each * ROWS
        tile = got[:, c // each, at : at + ROWS, :]
        tiles.append(tile.reshape(row_tiles * ROWS, LANES))
        rest.append(got[c // per, c % per, rows - TAIL :, :].astype(jnp.float32)[:3, :])
    return jnp.concatenate(tiles, axis=1), jnp.concatenate(rest, axis=1)


def softmax_sums(left, left_cols, right, right_scale, scores):
    height, width = left.shape[0], right.shape[1]
    step = 256

    def rows_of(k, r):
        return jnp.concatenate([left_cols[k, r : r + step, :]] * (width // LANES), axis=1)

    def fold(values, how):
        return how(values.reshape(step // 8, 8, width), axis=0)

    top = None
    for r in range(0, height, step):
        raw = jnp.dot(left[r : r + step, :], right, preferred_element_type=jnp.float32)
        part = raw * rows_of(0, r) * right_scale + rows_of(3, r)
        scores[r : r + step, :] = part
        best = fold(part, jnp.max)
        top = best if top is None else jnp.maximum(top, best)
    top = jnp.max(top, axis=0, keepdims=True)
    sums = [jnp.zeros((8, width), jnp.float32)] * 3
    for r in range(0, height, step):
        weight = jnp.exp2(scores[r : r + step, :] - top)
        parts = (weight, weight * rows_of(1, r), weight * rows_of(2, r))
        sums = [so_far + fold(part, jnp.sum) for so_far, part in zip(sums, parts)]
    return top, *(jnp.sum(part, axis=0, keepdims=True) for part in sums)


def column_kernel(factor, meta, left, left_cols, got, out, scores, packed):
    keypoints = left.shape[0]
    blocks = keypoints // LANES
    right, rest = column_block(got, 0, keypoints)
    top, total, spot_x, spot_y = softmax_sums(left, left_cols, right, rest[0:1] * factor, scores)
    lse = top + jnp.log2(total)
    for at, values in enumerate((lse, spot_x / total, spot_y / total)):
        for c in range(blocks):
            packed[at * blocks + c : at * blocks + c + 1, :] = values[:, c * LANES : (c + 1) * LANES]
    row = lax.broadcasted_iota(jnp.int32, packed.shape, 0)
    none = jnp.where(row < blocks, LOW, 0.0)
    for s in range(out.shape[0]):
        out[s] = jnp.where(meta[0:1, :] == s, packed[...], none)


def row_kernel(factor, meta, desc, attr, got, out, scores, left, left_cols):
    keypoints = desc.shape[1]
    for b in range(keypoints // 256):
        block, rest = column_block(got, b, 256)
        left[b * 256 : (b + 1) * 256, :] = block.astype(jnp.float32).T.astype(left.dtype)
        cols = jnp.concatenate([rest, jnp.zeros((5, 256), jnp.float32)], axis=0).T
        for k in range(3):
            left_cols[k, b * 256 : (b + 1) * 256, :] = jnp.broadcast_to(cols[:, k : k + 1], (256, LANES))
    row = lax.broadcasted_iota(jnp.int32, (keypoints, LANES), 0)
    left_cols[3] = jnp.where(row < meta[2:3, :], 0.0, LOW)
    for b in range(keypoints // 256):
        cut = slice(b * 256, (b + 1) * 256)
        scale = attr[0, 0:1, cut].astype(jnp.float32) * factor
        _, total, spot_x, spot_y = softmax_sums(left, left_cols, desc[:, cut], scale, scores)
        col = b * 256 + lax.broadcasted_iota(jnp.int32, (1, 256), 1)
        valid = col < meta[1:2, 0:1]
        out[0, 0:1, cut] = jnp.where(valid, spot_x / total, 0.0)
        out[0, 1:2, cut] = jnp.where(valid, spot_y / total, 0.0)


def merge_kernel(got, lse_out, xy_out):
    n, rows, _ = got.shape
    blocks = rows // 3
    lse = got[:, :blocks, :]
    peak = jnp.maximum(jnp.max(lse, axis=0), 0.0)
    share = jnp.exp2(lse - peak[None])
    partition = jnp.exp2(-peak) + jnp.sum(share, axis=0)
    log_total = (peak + jnp.log2(partition)) * math.log(2.0)
    x = jnp.sum(share * got[:, blocks : 2 * blocks, :], axis=0) / partition
    y = jnp.sum(share * got[:, 2 * blocks :, :], axis=0) / partition
    for c in range(blocks):
        cut = slice(c * LANES, (c + 1) * LANES)
        lse_out[0:1, cut] = log_total[c : c + 1]
        xy_out[0, 0:1, cut] = x[c : c + 1]
        xy_out[0, 1:2, cut] = y[c : c + 1]


def shards(descriptors, attributes, counts, owner_slot, pair_list):
    n = lax.axis_size("img")
    _, width, keypoints = descriptors.shape
    row_tiles, col_tiles = width // ROWS, keypoints // LANES
    each = row_tiles * col_tiles // n
    per = n // row_tiles
    rows = each * ROWS + TAIL
    factor = math.log2(math.e) / math.sqrt(width)
    bf16, f32 = jnp.bfloat16, jnp.float32
    desc = descriptors[0]
    share = functools.partial(
        lax.all_to_all, axis_name="img", split_axis=0, concat_axis=0, tiled=True
    )

    def call(*args, compiler_params=PARAMS, **kwargs):
        return pl.pallas_call(*args, compiler_params=compiler_params, **kwargs)

    shape = jax.ShapeDtypeStruct
    sent, meta = call(
        pack,
        out_shape=(pltpu.VMEM((row_tiles, per, rows, LANES), bf16), pltpu.VMEM((8, LANES), jnp.int32)),
        in_specs=[ANY] * 5,
        out_specs=(VMEM, VMEM),
        scratch_shapes=[
            pltpu.SMEM(pair_list.shape, jnp.int32),
            pltpu.SMEM(owner_slot.shape, jnp.int32),
            pltpu.SMEM(counts.shape, jnp.int32),
            pltpu.VMEM(attributes.shape, bf16),
            pltpu.SemaphoreType.DMA((4 + col_tiles,)),
        ],
        compiler_params=WIDE,
        name="pack",
    )(pair_list, owner_slot, counts, desc.reshape(row_tiles, ROWS, keypoints), attributes)
    spread = share(sent.reshape(n, rows, LANES))
    chosen = call(
        pick, out_shape=shape((n, rows, LANES), bf16), in_specs=[VMEM], out_specs=VMEM, name="pick"
    )(spread)
    partner = share(chosen).reshape(row_tiles, per, rows, LANES)
    left = desc.T
    here = lax.broadcasted_iota(jnp.int32, (keypoints, LANES), 0) < meta[1:2, :]
    left_cols = jnp.concatenate(
        [
            jnp.broadcast_to(attributes[0].astype(f32)[:, :, None], (3, keypoints, LANES)),
            jnp.where(here, 0.0, LOW)[None],
        ]
    )
    scores = pltpu.VMEM((keypoints, 256), f32)
    partials = call(
        functools.partial(column_kernel, factor),
        out_shape=pltpu.VMEM((n, 3 * col_tiles, LANES), f32),
        in_specs=[VMEM] * 4,
        out_specs=VMEM,
        scratch_shapes=[
            pltpu.VMEM((keypoints, keypoints), f32),
            pltpu.VMEM((3 * col_tiles, LANES), f32),
        ],
        name="columns",
    )(meta, left, left_cols, partner)
    arrived = share(partials)
    matched = call(
        functools.partial(row_kernel, factor),
        out_shape=shape((1, 2, keypoints), f32),
        in_specs=[VMEM] * 4,
        out_specs=VMEM,
        scratch_shapes=[
            scores,
            pltpu.VMEM((keypoints, width), bf16),
            pltpu.VMEM((4, keypoints, LANES), f32),
        ],
        cost_estimate=pl.CostEstimate(
            flops=2 * keypoints * keypoints * width,
            bytes_accessed=4 * keypoints * width,
            transcendentals=keypoints * keypoints,
        ),
        name="rows",
    )(meta, desc, attributes, partner)
    log_total, soft_xy = call(
        merge_kernel,
        out_shape=(shape((1, keypoints), f32), shape((1, 2, keypoints), f32)),
        in_specs=[VMEM],
        out_specs=(VMEM, VMEM),
        name="merge",
    )(arrived)
    return matched, log_total, soft_xy


def solution(mesh):
    both = ("groups", "img")
    return jax.shard_map(
        shards,
        mesh=mesh,
        in_specs=(P(both, None, None), P(both, None, None), P("groups"), P("groups"), P(both, None)),
        out_specs=(P(both, None, None), P(both, None), P(both, None, None)),
        check_vma=False,
    )
```
